32 devices in a mesh: section: 2 (over y), hid: 4 (over z), wid: 4 (over x, core).
Axes of the slice: x: 2, y: 2, z: 4, core: 2. Of those that a mesh axis runs over, the one named last changes fastest.
Arguments:
- weights: bfloat16 [2, 6144, 24576], P('section', 'hid', 'wid'), may hold values from -0.078125 to 0.078125
- preact: bfloat16 [1024, 24576], P(('section', 'hid'), 'wid'), may hold values from -6 to 6
- inputs: bfloat16 [1024, 6144], P(('section', 'wid'), 'hid'), may hold values from -6 to 6
- grad_out: bfloat16 [1024, 6144], P(('section', 'wid'), 'hid'), may hold values from -6 to 6
- row_state: float32 [2, 6144], P('section', 'hid'), may hold values from 32 to 256
- col_state: float32 [2, 24576], P('section', 'wid'), may hold values from 32 to 256
Outputs:
- input_grad: float32 [1024, 6144], P(('section', 'wid'), 'hid')
- update: float32 [2, 6144, 24576], P('section', 'hid', 'wid')
The draws below stay inside these ranges and needn't reach their ends.
All inputs are finite; a program needn't handle non-finite values.
Results may differ from the reference program's by a relative error of at most 0.0029.
Values may be sent and summed in bfloat16 or wider, within the bound.
A program may use at most 192 MiB of HBM per device.

```python
import math
import jax
import jax.numpy as jnp
from jax import lax

D = 6144
FF = 24576
TOKENS = 1024


def block_scale(rng, shape, cuts, low, top_value):
    factor_of, own = 1.0, jax.random.fold_in(rng, 6)
    for dim, parts in cuts:
        draws = jnp.exp(jax.random.uniform(jax.random.fold_in(own, dim), (parts,), jnp.float32, low / len(cuts), top_value / len(cuts)))
        factor_of = factor_of * jnp.repeat(draws, shape[dim] // parts).reshape([-1 if axis == dim else 1 for axis in range(len(shape))])
    return factor_of


def normal_values(key, extent, scale, bound, split=(), kind=jnp.bfloat16):
    drawn = jax.random.normal(key, extent, jnp.float32) * scale
    if len(split) > 0:
        drawn = block_scale(key, extent, split, -0.22, 0.18) * drawn
    return jnp.clip(drawn, min=-bound, max=bound).astype(kind)


def setup_inputs(seed: int = 0) -> dict:
    keys = jax.random.split(jax.random.key(seed), 7)
    return {
        "weights": normal_values(keys[0], (2, D, FF), D ** -0.5, 0.078125, ((0, 2), (1, 4), (2, 4))),
        "preact": normal_values(keys[1], (TOKENS, FF), 1.0, 6.0, ((0, 8), (1, 4))),
        "inputs": normal_values(keys[2], (TOKENS, D), 1.0, 6.0, ((0, 8), (1, 4))),
        "grad_out": normal_values(keys[3], (TOKENS, D), 1.0, 6.0, ((0, 8), (1, 4))),
        "row_state": jnp.clip(jnp.exp(math.log(256.0) - 2.0794415 * jax.random.uniform(keys[4], (2, D), jnp.float32) ** block_scale(keys[4], (2, D), ((0, 2), (1, 4)), -0.2, 0.2)), 32.0, 256.0),
        "col_state": jnp.clip(jnp.exp(math.log(256.0) - 2.0794415 * jax.random.uniform(keys[5], (2, FF), jnp.float32) ** block_scale(keys[5], (2, FF), ((0, 2), (1, 4)), -0.2, 0.2)), 32.0, 256.0),
    }


decay_rate = 0.9
root_half = 0.7071067811865476
inv_root_tau = 0.3989422804014327

def normal_cdf(pre):
    return 0.5 * (1.0 + lax.erf(pre * root_half))

def gelu_value(pre):
    return pre * normal_cdf(pre)

def gelu_slope(pre):
    return normal_cdf(pre) + pre * jnp.exp(-0.5 * pre * pre) * inv_root_tau

def factored_step(gradient, row_prev, col_prev):
    squares = gradient * gradient
    row_moment = decay_rate * row_prev + (1.0 - decay_rate) * lax.optimization_barrier(jnp.mean(squares, axis=1))
    col_moment = decay_rate * col_prev + (1.0 - decay_rate) * lax.optimization_barrier(jnp.mean(squares, axis=0))
    second = row_moment[:, None] * col_moment[None, :] / jnp.mean(row_moment)
    return gradient * lax.rsqrt(second)

def reference(weights, preact, inputs, grad_out, row_state, col_state):
    pre_float = preact.astype(jnp.float32)
    activation = gelu_value(pre_float).astype(jnp.bfloat16)
    down_grad = lax.dot_general(grad_out, activation, (((0,), (0,)), ((), ())), preferred_element_type=jnp.float32)
    hidden_grad = jnp.dot(grad_out, weights[1], preferred_element_type=jnp.float32)
    pre_grad = (hidden_grad * gelu_slope(pre_float)).astype(jnp.bfloat16)
    up_grad = lax.dot_general(inputs, pre_grad, (((0,), (0,)), ((), ())), preferred_element_type=jnp.float32)
    input_grad = lax.dot_general(pre_grad, weights[0], (((1,), (1,)), ((), ())), preferred_element_type=jnp.float32)
    input_grad = input_grad + grad_out.astype(jnp.float32)
    first_step = factored_step(up_grad, row_state[0], col_state[0])
    second_step = factored_step(down_grad, row_state[1], col_state[1])
    return (input_grad, jnp.stack([first_step, second_step]))
```

```python
import jax
import jax.numpy as jnp
from jax import lax
from jax.sharding import PartitionSpec as P

decay_rate = 0.9
root_half = 0.7071067811865476
inv_root_tau = 0.3989422804014327
LANES = 2
CUTS = 2


def normal_cdf(pre):
    return 0.5 * (1.0 + lax.erf(pre * root_half))


def gelu_value(pre):
    return pre * normal_cdf(pre)


def gelu_slope(pre):
    return normal_cdf(pre) + pre * jnp.exp(-0.5 * pre * pre) * inv_root_tau


def contract(left, right):
    return lax.dot_general(
        left, right, (((0,), (0,)), ((), ())), preferred_element_type=jnp.float32
    )


def chain_place(stream, pos, n):
    section, z = (1, pos) if pos < n else (0, 2 * n - 1 - pos)
    return section * n + (z if stream else n - 1 - z)


def shards(weights, preact, inputs, grad_out, row_state, col_state):
    n = lax.axis_size("hid")
    nw = lax.axis_size("wid")
    section = lax.axis_index("section")
    z = lax.axis_index("hid")
    w = lax.axis_index("wid")
    up = section == 0
    tile = weights[0]
    rows, width = preact.shape
    step_rows = rows // (LANES * CUTS)
    chunks = n * CUTS
    both = ("section", "hid")

    mine = jnp.where(up, inputs, grad_out)
    other = lax.ppermute(jnp.where(up, grad_out, inputs), "section", [(0, 1), (1, 0)])
    pair = jnp.stack([jnp.where(up, mine, other), jnp.where(up, other, mine)])
    left = lax.all_gather(pair, "wid", axis=1, tiled=True)
    depth = left.shape[-1]
    left = left.reshape(2, n, LANES, CUTS, step_rows, depth)
    halves = []
    for stream in (0, 1):
        order = range(n - 1, n // 2 - 1, -1) if stream else range(n // 2)
        picked = jnp.stack([left[s, k] for k in order for s in (1, 0)])
        halves.append(jnp.transpose(picked, (1, 0, 2, 3, 4)))
    left = jnp.stack(halves).reshape(-1, depth)
    part = jnp.dot(left, tile, preferred_element_type=jnp.float32)
    highest = jnp.where(up, 0.0, jnp.max(jnp.abs(part), axis=1))
    highest = lax.pmax(highest, "hid")
    scale = 16384.0 / jnp.maximum(n * highest, 1e-30)
    part = (part * scale[:, None]).astype(jnp.float16)
    part = part.reshape(2, LANES, chunks * step_rows, width)
    unscale = (1.0 / scale).reshape(2, LANES, chunks, step_rows, 1)

    total = 2 * LANES * chunks
    buf = jnp.zeros((total + 1, step_rows, width), jnp.bfloat16)

    def put_block(buf, block, s, at, valid):
        pieces = block.reshape(LANES, CUTS, step_rows, width)
        stream = at >= n // 2
        index = jnp.where(stream, n - 1 - at, at) * 2 + (1 - s)
        for lane in range(LANES):
            for cut in range(CUTS):
                base = (stream.astype(jnp.int32) * LANES + lane) * chunks + index * CUTS + cut
                slot = jnp.where(valid & (section == 1), base, total)
                buf = lax.dynamic_update_slice(buf, pieces[lane, cut][None], (slot, 0, 0))
        return buf

    def over_y(block):
        return lax.ppermute(block, "section", [(0, 1)])

    rightward = [(s * n + k, s * n + k + 1) for s in (0, 1) for k in range(n - 1)]
    leftward = [(b, a) for a, b in rightward]
    pre_own = preact
    pre_other = over_y(preact)
    pre_blocks = [[(pre_own, pre_other)], [(pre_own, pre_other)]]
    buf = put_block(buf, pre_own, 1, z, True)
    buf = put_block(buf, pre_other, 0, z, True)
    travel = [preact, preact]

    lanes = [(stream, lane) for stream in (0, 1) for lane in range(LANES)]
    pos = [
        jnp.where(up, 2 * n - 1 - (z if st else n - 1 - z), (z if st else n - 1 - z))
        for st in (0, 1)
    ]
    incoming = {key: None for key in lanes}
    carry = {key: None for key in lanes}

    def hops(st, places):
        return [(chain_place(st, q, n), chain_place(st, q + 1, n)) for q in places]

    ticks = chunks + 2 * n - 1
    spread = max(1, (chunks + n) // (n - 1)) if n > 1 else 1
    hop = 0
    for t in range(ticks):
        if hop < n - 1 and (t % spread == 0 or t == ticks - 1):
            hop += 1
            if carry[lanes[0]] is not None:
                tied = lax.optimization_barrier((travel, carry[lanes[0]]))
                travel, carry[lanes[0]] = list(tied[0]), tied[1]
            k = hop
            travel = [
                lax.ppermute(travel[0], both, [p for p in leftward if p[1] % n + k < n]),
                lax.ppermute(travel[1], both, [p for p in rightward if p[1] % n - k >= 0]),
            ]
            others = [over_y(block) for block in travel]
            for st in (0, 1):
                pre_blocks[st].append((travel[st], others[st]))
                at = z - k if st else z + k
                valid = (at >= 0) & (at < n)
                buf = put_block(buf, travel[st], 1, at, valid)
                buf = put_block(buf, others[st], 0, at, valid)
        for st, lane in lanes:
            got = incoming[st, lane]
            c = t - pos[st]
            if got is not None and t >= n:
                valid = up & (c >= 0) & (c < chunks)
                slot = jnp.where(valid, (st * LANES + lane) * chunks + c, total)
                buf = lax.dynamic_update_slice(buf, got[None], (slot, 0, 0))
            useful = [q for q in range(2 * n - 1) if 0 <= t - q < chunks]
            summing = [q for q in useful if q < n - 1]
            passing = [q for q in useful if q >= n - 1]
            at_end = t - (n - 1)
            sums = carry[st, lane]
            carry[st, lane] = incoming[st, lane] = None
            if summing or 0 <= at_end < chunks:
                start = jnp.clip(c, 0, chunks - 1) * step_rows
                value = lax.dynamic_slice(
                    part, (st, lane, start, 0), (1, 1, step_rows, width)
                )[0, 0].astype(jnp.float32)
                if sums is not None:
                    value = value + sums.astype(jnp.float32)
            if summing:
                carry[st, lane] = lax.ppermute(
                    value.astype(jnp.float16), both, hops(st, summing)
                )
            if passing:
                message = got
                if 0 <= at_end < chunks:
                    block, cut = divmod(at_end, CUTS)
                    pre = pre_blocks[st][block // 2][block % 2]
                    pre = pre.reshape(LANES, CUTS, step_rows, width)[lane, cut]
                    slope = gelu_slope(pre.astype(jnp.float32))
                    made = value * unscale[st, lane, at_end] * slope
                    message = made.astype(jnp.bfloat16)
                    if got is not None:
                        message = jnp.where(up, got, message)
                incoming[st, lane] = lax.ppermute(message, both, hops(st, passing))

    full = buf[:total].reshape(total * step_rows, width)

    share = lax.dot_general(
        full, tile, (((1,), (1,)), ((), ())), preferred_element_type=jnp.float32
    )
    share = share.reshape(2, LANES, n // 2, 2, CUTS, step_rows, depth)
    natural = [[None] * n, [None] * n]
    for stream in (0, 1):
        for i in range(n // 2):
            at = n - 1 - i if stream else i
            for j in (0, 1):
                natural[1 - j][at] = share[stream, :, i, j].reshape(rows, depth)
    share = jnp.stack([jnp.concatenate(half) for half in natural])
    tokens = grad_out.shape[0]
    share = share.reshape(2, nw, tokens, depth)
    summed = lax.dynamic_slice(share, (0, w, 0, 0), (2, 1, tokens, depth))[:, 0]
    wide = ("section", "wid")
    for d in range(1, nw):
        target = lax.rem(w + d, nw)
        out = lax.dynamic_slice(share, (0, target, 0, 0), (2, 1, tokens, depth))[:, 0]
        got = lax.ppermute(
            out.astype(jnp.bfloat16), wide, [(i, (i + d) % nw) for i in range(nw)]
        )
        summed = summed + got.astype(jnp.float32)
    across = lax.ppermute(summed[1], "section", [(0, 1)])
    input_grad = jnp.where(up, summed[0], across) + grad_out.astype(jnp.float32)

    right = jnp.where(up, full, gelu_value(full.astype(jnp.float32)).astype(jnp.bfloat16))
    gradient = contract(left, right)
    squares = gradient * gradient
    row_local = jnp.sum(squares, axis=1)
    col_local = jnp.sum(squares, axis=0)
    ff = width * nw
    d_model = depth * n
    row_total = lax.psum(row_local, "wid")
    row_moment = decay_rate * row_state[0] + (1.0 - decay_rate) / ff * row_total
    col_total, row_sum = lax.psum((col_local, jnp.sum(row_moment)), "hid")
    col_moment = decay_rate * col_state[0] + (1.0 - decay_rate) / d_model * col_total
    row_mean = row_sum / d_model
    update = gradient * lax.rsqrt(row_moment[:, None] * col_moment[None, :] / row_mean)
    return (input_grad, update[None])


def solution(mesh):
    placed = (
        P("section", "hid", "wid"),
        P(("section", "hid"), "wid"),
        P(("section", "wid"), "hid"),
        P(("section", "wid"), "hid"),
        P("section", "hid"),
        P("section", "wid"),
    )
    return jax.shard_map(
        shards,
        mesh=mesh,
        in_specs=placed,
        out_specs=(P(("section", "wid"), "hid"), P("section", "hid", "wid")),
        check_vma=False,
    )
```
